512 devices in a mesh: dp: 32 (over z, x), vocab: 16 (over y, core).
Axes of the slice: x: 4, y: 8, z: 8, core: 2. Of those that a mesh axis runs over, the one named last changes fastest.
Arguments:
- student_hidden: bfloat16 [16384, 4096], P(('dp', 'vocab')), may hold values from -16 to 16
- teacher_hidden: bfloat16 [16384, 4096], P(('dp', 'vocab')), may hold values from -16 to 16
- packing: int32 [16384], P(('dp', 'vocab')), may hold values from 0 to 16383, as said below
- token_mask: int32 [16384], P(('dp', 'vocab')), may hold values from 0 to 1
- student_head: bfloat16 [4096, 4096], P(None, 'vocab'), may hold values from -3 to 3
- teacher_head: bfloat16 [4096, 4096], P(None, 'vocab'), may hold values from -3 to 3
- loss_scale: float32 [], replicated, may hold values from 32768 to 131072
Outputs:
- hidden_grad: bfloat16 [16384, 4096], P(('dp', 'vocab'))
- loss: float32 [], replicated
The draws below stay inside these ranges and needn't reach their ends.
Inputs may be any that keep to these rules, and one draw needn't show every extreme that they name: At least one slot has token_mask 1. A permutation of the slots. Rollout row t and slot packing[t] lie on devices with the same vocab index (device of a row or slot: its index // 32, in dp-major order). Each device's rows go at most 2 to the devices of one dp index, and exactly 2 to one of them.
All inputs are finite; a program needn't handle non-finite values.
Results may differ from the reference program's by a relative error of at most 0.022.
Values may be sent and summed in bfloat16 or wider, within the bound.
No kernel may reach another device: no remote copies, remote signals or barrier semaphores. Data moves between devices by JAX's collectives and lax.ppermute only.
A program may use at most 64 MiB of HBM per device.

```python
import math
import jax
import jax.numpy as jnp
from jax import lax

D = 4096
VOC_DEV = 256
TOK_DEV = 32
VOCAB = 4096
TOKENS = 16384
CAP = 2
N_DP = 32
N_VOCAB = 16


def head_matrix(key, tag):
    key = jax.random.fold_in(key, tag)
    values = jnp.clip(jax.random.normal(key, (D, VOCAB), jnp.float32), -6.0, 6.0)
    return values * (3.0 * D ** (-0.5))


def hidden_rows(key):
    noise_key = jax.random.fold_in(key, 0)
    values = jnp.clip(jax.random.normal(noise_key, (TOKENS, D), jnp.float32), -6.0, 6.0)
    return jnp.clip(values, -16.0, 16.0)


def draw_student_head(key, part):
    return head_matrix(key, 101).astype(jnp.bfloat16)


def draw_teacher_head(key, part):
    return head_matrix(key, 202).astype(jnp.bfloat16)


def draw_student_hidden(key, part):
    key = jax.random.fold_in(key, 3)
    return hidden_rows(key).astype(jnp.bfloat16)


def draw_teacher_hidden(key, part):
    key = jax.random.fold_in(key, 4)
    return hidden_rows(key).astype(jnp.bfloat16)


def distinct_order(key, shape):
    width = shape[-1]
    scores = jax.random.randint(key, shape, 0, 1 << 20) * width + jnp.arange(width, dtype=jnp.int32)
    return jnp.argsort(scores, axis=-1).astype(jnp.int32)


def draw_packing(key, part):
    key = jax.random.fold_in(key, 7)
    keys = jax.random.split(key, 5)
    shared = jax.random.randint(keys[0], (N_VOCAB, 1), 0, N_DP)
    others = (shared + 1 + distinct_order(keys[1], (N_VOCAB, N_DP - 1))) % N_DP
    ranking = jnp.argsort(distinct_order(keys[2], (N_VOCAB, TOK_DEV)), axis=1).astype(jnp.int32)
    rest_index = jnp.maximum(ranking - CAP, 0) % (N_DP - 1)
    shift = jnp.where(ranking < CAP, shared, jnp.take_along_axis(others, rest_index, axis=1))
    group_order = distinct_order(keys[3], (N_VOCAB, N_DP))
    source = jnp.arange(N_DP, dtype=jnp.int32)[:, None, None]
    vocab_index = jnp.broadcast_to(jnp.arange(N_VOCAB, dtype=jnp.int32)[None, :, None], (N_DP, N_VOCAB, TOK_DEV))
    row_index = jnp.broadcast_to(jnp.arange(TOK_DEV, dtype=jnp.int32)[None, None, :], (N_DP, N_VOCAB, TOK_DEV))
    cyclic = (source + shift[None, :, :]) % N_DP
    target = group_order[vocab_index, cyclic]
    within = distinct_order(keys[4], (N_DP, N_VOCAB, TOK_DEV))
    slot_local = within[target, vocab_index, row_index]
    slots = (target * N_VOCAB + vocab_index) * TOK_DEV + slot_local
    return slots.reshape(TOKENS).astype(jnp.int32)


def draw_token_mask(key, part):
    key = jax.random.fold_in(key, 5)
    index = jnp.arange(TOKENS, dtype=jnp.int32)
    threshold = 250 + 500 * index // TOKENS
    picks = jax.random.randint(key, (TOKENS,), 0, 1000)
    return jnp.where((picks < threshold) | (index == 0), 1, 0).astype(jnp.int32)


def setup_inputs(seed: int = 0) -> dict:
    key_list = jax.random.split(jax.random.key(seed), 8)
    student_hidden = draw_student_hidden(jax.random.fold_in(key_list[7], 71), 0)
    teacher_hidden = draw_teacher_hidden(jax.random.fold_in(key_list[7], 71), 0)
    packing = draw_packing(jax.random.fold_in(key_list[7], 71), 0)
    token_mask = draw_token_mask(jax.random.fold_in(key_list[7], 71), 0)
    student_head = draw_student_head(jax.random.fold_in(key_list[7], 71), 0)
    teacher_head = draw_teacher_head(jax.random.fold_in(key_list[7], 71), 0)
    loss_scale = jnp.clip(jnp.exp(jax.random.uniform(key_list[6], (), jnp.float32, math.log(32768.0), math.log(131072.0))), 32768.0, 131072.0)
    return dict(student_hidden=student_hidden, teacher_hidden=teacher_hidden, packing=packing, token_mask=token_mask, student_head=student_head, teacher_head=teacher_head, loss_scale=loss_scale)


def log_normalizer(logits):
    top = jnp.max(logits, axis=1, keepdims=True)
    return top + jnp.log(jnp.sum(jnp.exp(logits - top), axis=1, keepdims=True))


def reference(student_hidden, teacher_hidden, packing, token_mask, student_head, teacher_head, loss_scale):
    placed = jnp.zeros_like(teacher_hidden).at[packing].set(teacher_hidden)
    student_logits = jnp.dot(student_hidden, student_head, preferred_element_type=jnp.float32)
    teacher_logits = jnp.dot(placed, teacher_head, preferred_element_type=jnp.float32)
    log_ps = student_logits - log_normalizer(student_logits)
    log_pt = teacher_logits - log_normalizer(teacher_logits)
    probs = jnp.exp(log_ps)
    row_kl = jnp.sum(probs * (log_ps - log_pt), axis=1)
    weights = token_mask.astype(jnp.float32)
    counted = jnp.sum(weights)
    loss = jnp.sum(weights * row_kl) / counted
    factor = loss_scale * weights / counted
    logit_grad = (factor[:, None] * probs * (log_ps - log_pt - row_kl[:, None])).astype(jnp.bfloat16)

    def add_block(total, block):
        begin = (block * VOC_DEV).astype(jnp.int32)
        grad_part = lax.dynamic_slice_in_dim(logit_grad, begin, VOC_DEV, 1)
        head_part = lax.dynamic_slice_in_dim(student_head, begin, VOC_DEV, 1)
        partial_sum = lax.dot_general(grad_part, head_part, (((1,), (1,)), ((), ())), preferred_element_type=jnp.float32)
        rounded = lax.optimization_barrier(partial_sum.astype(jnp.bfloat16))
        return total + rounded.astype(jnp.float32), None

    start_total = jnp.zeros((TOKENS, D), jnp.float32)
    total, unused = lax.scan(add_block, start_total, jnp.arange(N_VOCAB, dtype=jnp.int32))
    return total.astype(jnp.bfloat16), loss
```

```python
import jax
import jax.numpy as jnp
from jax import lax
from jax.sharding import Mesh, PartitionSpec as P

BF = jnp.bfloat16
F32 = jnp.float32
CORES = 2


def dot(a, b, ca, cb):
    return lax.dot_general(a, b, (((ca,), (cb,)), ((), ())), preferred_element_type=F32)


def exchange(x, axis):
    return lax.all_to_all(x, axis, split_axis=0, concat_axis=0, tiled=True)


def body(student_hidden, teacher_hidden, packing, token_mask, student_head, teacher_head, loss_scale):
    tok, width = student_hidden.shape
    n_dp, n_y = lax.axis_size("dp"), lax.axis_size("y")
    cap = max(2, 2 * tok // n_dp)
    rows = n_y * tok
    swap = [(0, 1), (1, 0)]

    student_rows = exchange(
        jnp.broadcast_to(student_hidden[None], (n_y, tok, width)), "y"
    ).reshape(rows, width)

    destination = packing // (n_y * CORES * tok)
    local = packing % tok
    index = jnp.arange(tok, dtype=jnp.int32)
    earlier = (destination[:, None] == destination[None, :]) & (index[None, :] < index[:, None])
    rank = jnp.sum(earlier.astype(jnp.int32), axis=1)
    position = destination * cap + rank
    spread = (jnp.arange(n_dp * cap, dtype=jnp.int32)[:, None] == position[None, :]).astype(BF)
    payload = jnp.concatenate(
        [teacher_hidden, jnp.broadcast_to((local + 1).astype(BF)[:, None], (tok, 128))], axis=1
    )
    send = dot(spread, payload, 1, 0).astype(BF)
    got = exchange(send.reshape(n_dp, cap, width + 128), "dp").reshape(n_dp * cap, width + 128)
    slots = got[:, width].astype(jnp.int32) - 1
    place = (lax.rem(jnp.arange(rows, dtype=jnp.int32), tok)[:, None] == slots[None, :]).astype(BF)
    placed = dot(place, got[:, :width], 1, 0).astype(BF)
    teacher_rows = exchange(placed.reshape(n_y, tok, width), "y").reshape(rows, width)

    student_both = jnp.concatenate(
        [student_head, lax.ppermute(student_head, "core", swap)], axis=1
    )
    teacher_both = jnp.concatenate(
        [teacher_head, lax.ppermute(teacher_head, "core", swap)], axis=1
    )

    student_logits = dot(student_rows, student_both, 1, 0)
    teacher_logits = dot(teacher_rows, teacher_both, 1, 0)
    difference = student_logits - teacher_logits
    student_top = jnp.max(student_logits, axis=1)
    teacher_top = jnp.max(teacher_logits, axis=1)
    student_exp = jnp.exp(student_logits - student_top[:, None])
    teacher_exp = jnp.exp(teacher_logits - teacher_top[:, None])
    own_mask = jnp.pad(token_mask.astype(F32), (0, rows - tok))
    stats = jnp.stack(
        [
            student_top,
            teacher_top,
            jnp.sum(student_exp, axis=1),
            jnp.sum(teacher_exp, axis=1),
            jnp.sum(student_exp * difference, axis=1),
            own_mask,
        ]
    )
    stats = exchange(jnp.broadcast_to(stats[None], (n_y,) + stats.shape), "y")
    student_max = jnp.max(stats[:, 0], axis=0)
    teacher_max = jnp.max(stats[:, 1], axis=0)
    student_scale = jnp.exp(stats[:, 0] - student_max[None])
    teacher_scale = jnp.exp(stats[:, 1] - teacher_max[None])
    student_sum = jnp.sum(stats[:, 2] * student_scale, axis=0)
    teacher_sum = jnp.sum(stats[:, 3] * teacher_scale, axis=0)
    mean_difference = jnp.sum(stats[:, 4] * student_scale, axis=0) / student_sum
    row_kl = (
        mean_difference
        - (student_max + jnp.log(student_sum))
        + (teacher_max + jnp.log(teacher_sum))
    )
    weights = stats[:, 5, :tok].reshape(rows)

    parts = jnp.stack([jnp.sum(weights * row_kl), jnp.sum(weights)])
    parts = jnp.broadcast_to(jnp.pad(parts, (0, 126))[None, None], (n_dp * CORES, 1, 128))
    totals = jnp.sum(exchange(parts, ("dp", "core")), axis=(0, 1))
    counted = totals[1]
    loss = totals[0] / counted

    probs = jnp.exp(student_logits - student_max[:, None]) / student_sum[:, None]
    grad = (probs * (difference - mean_difference[:, None])).astype(BF)
    partial = dot(grad, student_both, 1, 1).astype(BF)
    blocks = exchange(partial.reshape(n_y, tok, width), "y")
    factor = loss_scale * token_mask.astype(F32) / counted
    hidden_grad = (factor[:, None] * jnp.sum(blocks.astype(F32), axis=0)).astype(BF)
    return hidden_grad, loss


def solution(mesh):
    dp, vocab = mesh.devices.shape
    grid = Mesh(mesh.devices.reshape(dp, vocab // CORES, CORES), ("dp", "y", "core"))
    every = ("dp", "y", "core")
    return jax.shard_map(
        body,
        mesh=grid,
        in_specs=(
            P(every, None),
            P(every, None),
            P(every),
            P(every),
            P(None, ("y", "core")),
            P(None, ("y", "core")),
            P(),
        ),
        out_specs=(P(every, None), P()),
        check_vma=False,
    )
```

```python
import jax
import jax.numpy as jnp
from jax import lax
from jax.sharding import Mesh, PartitionSpec as P

BF = jnp.bfloat16
F32 = jnp.float32
CORES = 2


def dot(a, b, ca, cb):
    return lax.dot_general(a, b, (((ca,), (cb,)), ((), ())), preferred_element_type=F32)


def exchange(x, axis):
    return lax.all_to_all(x, axis, split_axis=0, concat_axis=0, tiled=True)


def ring_gather(x, axis):
    n = lax.axis_size(axis)
    me = lax.axis_index(axis)
    right = [(i, (i + 1) % n) for i in range(n)]
    left = [(i, (i - 1) % n) for i in range(n)]
    half = x.shape[0] // 2
    out = jnp.zeros((n,) + x.shape, x.dtype)

    def put(out, block, owner, row=0):
        return lax.dynamic_update_slice(out, block[None], (lax.rem(owner, n), row, 0))

    out = put(out, x, me)
    r = l = x
    for k in range(1, n // 2):
        r = lax.ppermute(r, axis, right)
        l = lax.ppermute(l, axis, left)
        out = put(out, r, me + n - k)
        out = put(out, l, me + k)
    r = lax.ppermute(r[:half], axis, right)
    l = lax.ppermute(l[half:], axis, left)
    out = put(out, r, me + n // 2)
    return put(out, l, me + n // 2, half)


def body(student_hidden, teacher_hidden, packing, token_mask, student_head, teacher_head, loss_scale):
    tok, width = student_hidden.shape
    n_dp, n_y = lax.axis_size("dp"), lax.axis_size("y")
    cap = max(2, 2 * tok // n_dp)
    rows = n_y * tok
    swap = [(0, 1), (1, 0)]

    student_rows = lax.all_gather(student_hidden, "y", axis=0, tiled=True)

    destination = packing // (n_y * CORES * tok)
    local = packing % tok
    index = jnp.arange(tok, dtype=jnp.int32)
    earlier = (destination[:, None] == destination[None, :]) & (index[None, :] < index[:, None])
    rank = jnp.sum(earlier.astype(jnp.int32), axis=1)
    position = destination * cap + rank
    spread = (jnp.arange(n_dp * cap, dtype=jnp.int32)[:, None] == position[None, :]).astype(BF)
    payload = jnp.concatenate(
        [teacher_hidden, jnp.broadcast_to((local + 1).astype(BF)[:, None], (tok, 128))], axis=1
    )
    send = dot(spread, payload, 1, 0).astype(BF)
    got = exchange(send.reshape(n_dp, cap, width + 128), "dp").reshape(n_dp * cap, width + 128)
    slots = got[:, width].astype(jnp.int32) - 1
    place = (index[:, None] == slots[None, :]).astype(BF)
    placed = dot(place, got[:, :width], 1, 0).astype(BF)
    teacher_rows = ring_gather(placed, "y").reshape(rows, width)

    student_both = jnp.concatenate(
        [student_head, lax.ppermute(student_head, "core", swap)], axis=1
    )
    teacher_both = jnp.concatenate(
        [teacher_head, lax.ppermute(teacher_head, "core", swap)], axis=1
    )

    student_logits = dot(student_rows, student_both, 1, 0)
    teacher_logits = dot(teacher_rows, teacher_both, 1, 0)
    difference = student_logits - teacher_logits
    student_top = jnp.max(student_logits, axis=1)
    teacher_top = jnp.max(teacher_logits, axis=1)
    student_exp = jnp.exp(student_logits - student_top[:, None])
    teacher_exp = jnp.exp(teacher_logits - teacher_top[:, None])
    own_mask = jnp.pad(token_mask.astype(F32), (0, rows - tok))
    stats = jnp.stack(
        [
            student_top,
            teacher_top,
            jnp.sum(student_exp, axis=1),
            jnp.sum(teacher_exp, axis=1),
            jnp.sum(student_exp * difference, axis=1),
            own_mask,
        ]
    )
    stats = exchange(jnp.broadcast_to(stats[None], (n_y,) + stats.shape), "y")
    student_max = jnp.max(stats[:, 0], axis=0)
    teacher_max = jnp.max(stats[:, 1], axis=0)
    student_scale = jnp.exp(stats[:, 0] - student_max[None])
    teacher_scale = jnp.exp(stats[:, 1] - teacher_max[None])
    student_sum = jnp.sum(stats[:, 2] * student_scale, axis=0)
    teacher_sum = jnp.sum(stats[:, 3] * teacher_scale, axis=0)
    mean_difference = jnp.sum(stats[:, 4] * student_scale, axis=0) / student_sum
    row_kl = (
        mean_difference
        - (student_max + jnp.log(student_sum))
        + (teacher_max + jnp.log(teacher_sum))
    )
    weights = stats[:, 5, :tok].reshape(rows)

    probs = jnp.exp(student_logits - student_max[:, None]) / student_sum[:, None]
    grad = (probs * (difference - mean_difference[:, None])).astype(BF)
    partial = dot(grad, student_both, 1, 1).astype(BF)
    summed = lax.psum_scatter(partial, "y", scatter_dimension=0, tiled=True)

    parts = jnp.stack([jnp.sum(weights * row_kl), jnp.sum(weights)])
    parts = jnp.broadcast_to(jnp.pad(parts, (0, 126))[None, None], (n_dp * CORES, 1, 128))
    totals = jnp.sum(exchange(parts, ("dp", "core")), axis=(0, 1))
    counted = totals[1]
    loss = totals[0] / counted
    factor = loss_scale * token_mask.astype(F32) / counted
    hidden_grad = (factor[:, None] * summed.astype(F32)).astype(BF)
    return hidden_grad, loss


def solution(mesh):
    dp, vocab = mesh.devices.shape
    grid = Mesh(mesh.devices.reshape(dp, vocab // CORES, CORES), ("dp", "y", "core"))
    every = ("dp", "y", "core")
    return jax.shard_map(
        body,
        mesh=grid,
        in_specs=(
            P(every, None),
            P(every, None),
            P(every),
            P(every),
            P(None, ("y", "core")),
            P(None, ("y", "core")),
            P(),
        ),
        out_specs=(P(every, None), P()),
        check_vma=False,
    )
```

```python
import jax
import jax.experimental.pallas as pl
import jax.experimental.pallas.tpu as pltpu
import jax.numpy as jnp
from jax import lax
from jax.sharding import Mesh, PartitionSpec as P

BF = jnp.bfloat16
F32 = jnp.float32
CORES = 2
STATS = 8
STEPS = 4
GRADIENT_STEPS = 2
VMEM_LIMIT = 16 * 1024 * 1024


def dot(a, b, ca, cb):
    return lax.dot_general(a, b, (((ca,), (cb,)), ((), ())), preferred_element_type=F32)


def exchange(x, axis):
    return lax.all_to_all(x, axis, split_axis=0, concat_axis=0, tiled=True)


def ring_gather(x, out, axis, beside):
    n = lax.axis_size(axis)
    me = lax.axis_index(axis)
    right = [(i, (i + 1) % n) for i in range(n)]
    left = [(i, (i - 1) % n) for i in range(n)]
    half = x.shape[0] // 2

    def put(out, block, owner, row=0):
        return lax.dynamic_update_slice(out, block[None], (lax.rem(owner, n), row, 0))

    out = put(out, x, me)
    r = l = x
    for k in range(1, n // 2):
        r = lax.ppermute(r, axis, right)
        l = lax.ppermute(l, axis, left)
        out = put(out, r, me + n - k)
        out = put(out, l, me + k)
        if k == 2:
            r, l, beside = lax.optimization_barrier((r, l, beside))
    r = lax.ppermute(r[:half], axis, right)
    l = lax.ppermute(l[half:], axis, left)
    out = put(out, r, me + n // 2)
    return put(out, l, me + n // 2, half), beside


def buffers(*shapes):
    return pl.pallas_call(
        lambda *refs: None,
        out_specs=[pl.BlockSpec(memory_space=pl.ANY) for _ in shapes],
        out_shape=[pltpu.HBM(shape, BF) for shape in shapes],
        name="buffers",
    )()


def logits_kernel(xs_ref, xt_ref, ws0_ref, ws1_ref, wt0_ref, wt1_ref, mask_ref, s_ref, d_ref, stats_ref):
    step = pl.program_id(0)
    rows, block = s_ref.shape[0], ws0_ref.shape[1]
    xs = xs_ref[...].reshape(rows, xs_ref.shape[2])
    xt = xt_ref[...].reshape(rows, xt_ref.shape[2])

    @pl.when(step == 0)
    def _():
        s_ref[...] = jnp.zeros_like(s_ref)
        d_ref[...] = jnp.zeros_like(d_ref)

    s_ref[:, :block] += dot(xs, ws0_ref[...], 1, 0)
    s_ref[:, block:] += dot(xs, ws1_ref[...], 1, 0)
    d_ref[:, :block] += dot(xt, wt0_ref[...], 1, 0)
    d_ref[:, block:] += dot(xt, wt1_ref[...], 1, 0)

    @pl.when(step == pl.num_programs(0) - 1)
    def _():
        s, t = s_ref[...], d_ref[...]
        d = s - t
        d_ref[...] = d
        s_top = jnp.max(s, axis=1, keepdims=True)
        t_top = jnp.max(t, axis=1, keepdims=True)
        e = jnp.exp(s - s_top)
        columns = (
            s_top,
            t_top,
            jnp.sum(e, axis=1, keepdims=True),
            jnp.sum(jnp.exp(t - t_top), axis=1, keepdims=True),
            jnp.sum(e * d, axis=1, keepdims=True),
        )
        lane = lax.broadcasted_iota(jnp.int32, (rows, 128), 1)
        table = jnp.zeros((rows, 128), F32)
        for j, column in enumerate(columns):
            table = jnp.where(lane == j, column, table)
        table = table.T[:STATS]
        line = lax.broadcasted_iota(jnp.int32, (STATS, rows), 0)
        table = jnp.where(line == len(columns), mask_ref[...], table)
        stats_ref[...] = jnp.broadcast_to(table[None], stats_ref.shape)


def logits(student_rows, teacher_rows, heads, mask):
    n_y, tok, width = student_rows.shape
    rows = n_y * tok
    block = heads[0].shape[1]
    depth = width // STEPS
    head = pl.BlockSpec((depth, block), lambda k: (k, 0))
    whole = pl.BlockSpec((rows, CORES * block), lambda k: (0, 0))
    return pl.pallas_call(
        logits_kernel,
        grid=(STEPS,),
        in_specs=[
            pl.BlockSpec((n_y, tok, depth), lambda k: (0, 0, k)),
            pl.BlockSpec((n_y, tok, depth), lambda k: (0, 0, k)),
            head,
            head,
            head,
            head,
            pl.BlockSpec((1, rows), lambda k: (0, 0)),
        ],
        out_specs=[whole, whole, pl.BlockSpec((n_y, STATS, rows), lambda k: (0, 0, 0))],
        out_shape=[
            jax.ShapeDtypeStruct((rows, CORES * block), F32),
            jax.ShapeDtypeStruct((rows, CORES * block), F32),
            jax.ShapeDtypeStruct((n_y, STATS, rows), F32),
        ],
        compiler_params=pltpu.CompilerParams(vmem_limit_bytes=VMEM_LIMIT),
        cost_estimate=pl.CostEstimate(
            flops=8 * rows * width * block, bytes_accessed=12 * 2**20, transcendentals=2**18
        ),
        name="logits",
    )(student_rows, teacher_rows, *heads, mask)


def gradient_kernel(stats_ref, s_ref, d_ref, w0_ref, w1_ref, out_ref, parts_ref, grad_ref):
    rows, block = s_ref.shape[0], w0_ref.shape[1]

    @pl.when(pl.program_id(0) == 0)
    def _():
        stats = [stats_ref[:, j, :] for j in range(6)]
        s_top = jnp.max(stats[0], axis=0, keepdims=True)
        t_top = jnp.max(stats[1], axis=0, keepdims=True)
        scale = jnp.exp(stats[0] - s_top)
        s_sum = jnp.sum(stats[2] * scale, axis=0, keepdims=True)
        t_sum = jnp.sum(stats[3] * jnp.exp(stats[1] - t_top), axis=0, keepdims=True)
        mean = jnp.sum(stats[4] * scale, axis=0, keepdims=True) / s_sum
        weights = jnp.sum(stats[5], axis=0, keepdims=True)
        row_kl = mean - (s_top + jnp.log(s_sum)) + (t_top + jnp.log(t_sum))
        lane = lax.broadcasted_iota(jnp.int32, parts_ref.shape, 1)
        parts_ref[...] = jnp.where(
            lane == 0, jnp.sum(weights * row_kl), jnp.where(lane == 1, jnp.sum(weights), 0.0)
        )
        line = lax.broadcasted_iota(jnp.int32, (128, rows), 0)
        table = jnp.where(line == 0, s_top, jnp.where(line == 1, 1.0 / s_sum, mean)).T
        probs = jnp.exp(s_ref[...] - table[:, 0:1]) * table[:, 1:2]
        grad_ref[...] = (probs * (d_ref[...] - table[:, 2:3])).astype(BF)

    out_ref[...] = (
        dot(grad_ref[:, :block], w0_ref[...], 1, 1) + dot(grad_ref[:, block:], w1_ref[...], 1, 1)
    ).astype(BF)


def gradient(stats, s, d, heads, copies):
    rows, (width, block) = s.shape[0], heads[0].shape
    depth = width // GRADIENT_STEPS
    head = pl.BlockSpec((depth, block), lambda k: (k, 0))
    whole = pl.BlockSpec(s.shape, lambda k: (0, 0))
    return pl.pallas_call(
        gradient_kernel,
        grid=(GRADIENT_STEPS,),
        in_specs=[pl.BlockSpec(stats.shape, lambda k: (0, 0, 0)), whole, whole, head, head],
        out_specs=[
            pl.BlockSpec((rows, depth), lambda k: (0, k)),
            pl.BlockSpec((copies, 128), lambda k: (0, 0)),
        ],
        out_shape=[
            pltpu.HBM((rows, width), BF),
            jax.ShapeDtypeStruct((copies, 128), F32),
        ],
        scratch_shapes=[pltpu.VMEM(s.shape, BF)],
        compiler_params=pltpu.CompilerParams(vmem_limit_bytes=VMEM_LIMIT),
        cost_estimate=pl.CostEstimate(
            flops=4 * rows * width * block, bytes_accessed=7 * 2**20, transcendentals=2**17
        ),
        name="gradient",
    )(stats, s, d, *heads)


def body(student_hidden, teacher_hidden, packing, token_mask, student_head, teacher_head, loss_scale):
    tok, width = student_hidden.shape
    n_dp, n_y = lax.axis_size("dp"), lax.axis_size("y")
    cap = max(2, 2 * tok // n_dp)
    rows = n_y * tok
    swap = [(0, 1), (1, 0)]

    destination = packing // (n_y * CORES * tok)
    local = packing % tok
    index = jnp.arange(tok, dtype=jnp.int32)
    earlier = (destination[:, None] == destination[None, :]) & (index[None, :] < index[:, None])
    rank = jnp.sum(earlier.astype(jnp.int32), axis=1)
    position = destination * cap + rank
    payload = jnp.concatenate(
        [teacher_hidden, jnp.broadcast_to((local + 1).astype(BF)[:, None], (tok, 128))], axis=1
    )

    def teacher_turn(_, carry):
        position, out, *_ = carry
        spread = (jnp.arange(n_dp * cap, dtype=jnp.int32)[:, None] == position[None, :]).astype(BF)
        send = dot(spread, payload, 1, 0).astype(BF)
        got = exchange(send.reshape(n_dp, cap, width + 128), "dp").reshape(n_dp * cap, width + 128)
        slots = got[:, width].astype(jnp.int32) - 1
        place = (index[:, None] == slots[None, :]).astype(BF)
        placed = dot(place, got[:, :width], 1, 0).astype(BF)
        heads, placed = lax.optimization_barrier(((student_head, teacher_head), placed))
        other = [lax.ppermute(head, "core", swap) for head in heads]
        out, other = ring_gather(placed, out, "y", other)
        return slots[:tok], out, *other

    student_rows = lax.all_gather(student_hidden, "y", axis=0)
    once = lax.optimization_barrier(jnp.int32(1))
    empty = buffers((n_y, tok, width), student_head.shape, teacher_head.shape)
    _, teacher_rows, *other = lax.fori_loop(0, once, teacher_turn, (position, *empty))

    mine = jnp.arange(rows, dtype=jnp.int32) // tok == lax.axis_index("y")
    mask = jnp.where(mine, jnp.tile(token_mask.astype(F32), n_y), 0.0)[None]

    student_rows, teacher_rows, teacher_head = (
        pltpu.with_memory_space_constraint(x, pltpu.HBM) for x in (student_rows, teacher_rows, teacher_head)
    )
    s, d, stats = logits(student_rows, teacher_rows, (student_head, other[0], teacher_head, other[1]), mask)
    stats = exchange(stats, "y")
    partial, parts = gradient(stats, s, d, (student_head, other[0]), n_dp * CORES)
    summed = lax.psum_scatter(partial, "y", scatter_dimension=0, tiled=True)

    totals = jnp.sum(exchange(parts[:, None], ("dp", "core")), axis=(0, 1))
    counted = totals[1]
    loss = totals[0] / counted
    factor = loss_scale * token_mask.astype(F32) / counted
    hidden_grad = (factor[:, None] * summed.astype(F32)).astype(BF)
    return hidden_grad, loss


def solution(mesh):
    dp, vocab = mesh.devices.shape
    grid = Mesh(mesh.devices.reshape(dp, vocab // CORES, CORES), ("dp", "y", "core"))
    every = ("dp", "y", "core")
    return jax.shard_map(
        body,
        mesh=grid,
        in_specs=(
            P(every, None),
            P(every, None),
            P(every),
            P(every),
            P(None, ("y", "core")),
            P(None, ("y", "core")),
            P(),
        ),
        out_specs=(P(every, None), P()),
        check_vma=False,
    )
```

```python
import jax
import jax.experimental.pallas as pl
import jax.experimental.pallas.tpu as pltpu
import jax.numpy as jnp
from jax import lax
from jax.sharding import Mesh, PartitionSpec as P

BF = jnp.bfloat16
F32 = jnp.float32
CORES = 2
STATS = 8
STEPS = 4
LOGITS_VMEM = 32 * 1024 * 1024
GRADIENT_STEPS = 2
VMEM_LIMIT = 16 * 1024 * 1024


def dot(a, b, ca, cb):
    return lax.dot_general(a, b, (((ca,), (cb,)), ((), ())), preferred_element_type=F32)


def exchange(x, axis):
    return lax.all_to_all(x, axis, split_axis=0, concat_axis=0, tiled=True)


def ring_gather(x, out, axis, beside):
    n = lax.axis_size(axis)
    me = lax.axis_index(axis)
    right = [(i, (i + 1) % n) for i in range(n)]
    left = [(i, (i - 1) % n) for i in range(n)]
    half = x.shape[0] // 2

    def put(out, block, owner, row=0):
        return lax.dynamic_update_slice(out, block[None], (lax.rem(owner, n), row, 0))

    out = put(out, x, me)
    r = l = x
    for k in range(1, n // 2):
        r = lax.ppermute(r, axis, right)
        l = lax.ppermute(l, axis, left)
        out = put(out, r, me + n - k)
        out = put(out, l, me + k)
        if k == 2:
            r, l, beside = lax.optimization_barrier((r, l, beside))
    r = lax.ppermute(r[:half], axis, right)
    l = lax.ppermute(l[half:], axis, left)
    out = put(out, r, me + n // 2)
    return put(out, l, me + n // 2, half), beside


def buffers(*shapes):
    return pl.pallas_call(
        lambda *refs: None,
        out_specs=[pl.BlockSpec(memory_space=pl.ANY) for _ in shapes],
        out_shape=[pltpu.HBM(shape, BF) for shape in shapes],
        name="buffers",
    )()


def logits_kernel(xs, xt, ws0, ws1, wt0, wt1, mask_ref, s_ref, d_ref, stats_ref, *scratch):
    *held, sems = scratch
    n_y, tok, width = xs.shape
    rows, block = n_y * tok, ws0.shape[1]
    depth = width // STEPS

    def copies(side, k):
        part = pl.ds(k * depth, depth)
        for j, ref in enumerate(((xs, ws0, ws1), (xt, wt0, wt1))[side]):
            at = (slice(None), slice(None), part) if j == 0 else (part, slice(None))
            yield pltpu.make_async_copy(ref.at[at], held[3 * side + j].at[at], sems.at[3 * side + j, k])

    for side in range(2):
        for k in range(STEPS):
            for copy in copies(side, k):
                copy.start()

    def product(side, out_ref):
        x, w0, w1 = held[3 * side : 3 * side + 3]
        for k in range(STEPS):
            for copy in copies(side, k):
                copy.wait()
            part = pl.ds(k * depth, depth)
            rows_in = x[:, :, part].reshape(rows, depth)
            p0, p1 = dot(rows_in, w0[part, :], 1, 0), dot(rows_in, w1[part, :], 1, 0)
            if k == 0:
                out_ref[:, :block] = p0
                out_ref[:, block:] = p1
            else:
                out_ref[:, :block] += p0
                out_ref[:, block:] += p1

    product(0, s_ref)
    s = s_ref[...]
    s_top = jnp.max(s, axis=1, keepdims=True)
    s_sum = jnp.sum(jnp.exp(s - s_top), axis=1, keepdims=True)
    product(1, d_ref)
    s, t = s_ref[...], d_ref[...]
    d = s - t
    d_ref[...] = d
    t_top = jnp.max(t, axis=1, keepdims=True)
    t_sum = jnp.sum(jnp.exp(t - t_top), axis=1, keepdims=True)
    cross = jnp.sum(jnp.exp(s - s_top) * d, axis=1, keepdims=True)
    columns = (s_top, t_top, s_sum, t_sum, cross)
    lane = lax.broadcasted_iota(jnp.int32, (rows, 128), 1)
    table = jnp.zeros((rows, 128), F32)
    for j, column in enumerate(columns):
        table = jnp.where(lane == j, column, table)
    table = table.T[:STATS]
    line = lax.broadcasted_iota(jnp.int32, (STATS, rows), 0)
    table = jnp.where(line == len(columns), mask_ref[...], table)
    stats_ref[...] = jnp.broadcast_to(table[None], stats_ref.shape)


def logits(student_rows, teacher_rows, heads, mask):
    n_y, tok, width = student_rows.shape
    rows, block = n_y * tok, heads[0].shape[1]
    far, near = pl.BlockSpec(memory_space=pltpu.HBM), pl.BlockSpec(memory_space=pltpu.VMEM)
    side = [pltpu.VMEM(student_rows.shape, BF), pltpu.VMEM((width, block), BF), pltpu.VMEM((width, block), BF)]
    return pl.pallas_call(
        logits_kernel,
        in_specs=[far] * 6 + [near],
        out_specs=[near] * 3,
        out_shape=[
            jax.ShapeDtypeStruct((rows, CORES * block), F32),
            jax.ShapeDtypeStruct((rows, CORES * block), F32),
            jax.ShapeDtypeStruct((n_y, STATS, rows), F32),
        ],
        scratch_shapes=side + side + [pltpu.SemaphoreType.DMA((6, STEPS))],
        compiler_params=pltpu.CompilerParams(vmem_limit_bytes=LOGITS_VMEM),
        cost_estimate=pl.CostEstimate(
            flops=8 * rows * width * block, bytes_accessed=12 * 2**20, transcendentals=2**18
        ),
        name="logits",
    )(*(pltpu.with_memory_space_constraint(x, pltpu.HBM) for x in (student_rows, teacher_rows, *heads)), mask)


def gradient_kernel(stats_ref, s_ref, d_ref, w0_ref, w1_ref, out_ref, parts_ref, grad_ref):
    rows, block = s_ref.shape[0], w0_ref.shape[1]

    @pl.when(pl.program_id(0) == 0)
    def _():
        stats = [stats_ref[:, j, :] for j in range(6)]
        s_top = jnp.max(stats[0], axis=0, keepdims=True)
        t_top = jnp.max(stats[1], axis=0, keepdims=True)
        scale = jnp.exp(stats[0] - s_top)
        s_sum = jnp.sum(stats[2] * scale, axis=0, keepdims=True)
        t_sum = jnp.sum(stats[3] * jnp.exp(stats[1] - t_top), axis=0, keepdims=True)
        mean = jnp.sum(stats[4] * scale, axis=0, keepdims=True) / s_sum
        weights = jnp.sum(stats[5], axis=0, keepdims=True)
        row_kl = mean - (s_top + jnp.log(s_sum)) + (t_top + jnp.log(t_sum))
        lane = lax.broadcasted_iota(jnp.int32, parts_ref.shape, 1)
        parts_ref[...] = jnp.where(
            lane == 0, jnp.sum(weights * row_kl), jnp.where(lane == 1, jnp.sum(weights), 0.0)
        )
        line = lax.broadcasted_iota(jnp.int32, (128, rows), 0)
        table = jnp.where(line == 0, s_top, jnp.where(line == 1, 1.0 / s_sum, mean)).T
        probs = jnp.exp(s_ref[...] - table[:, 0:1]) * table[:, 1:2]
        grad_ref[...] = (probs * (d_ref[...] - table[:, 2:3])).astype(BF)

    out_ref[...] = (
        dot(grad_ref[:, :block], w0_ref[...], 1, 1) + dot(grad_ref[:, block:], w1_ref[...], 1, 1)
    ).astype(BF)


def gradient(stats, s, d, heads, copies):
    rows, (width, block) = s.shape[0], heads[0].shape
    depth = width // GRADIENT_STEPS
    head = pl.BlockSpec((depth, block), lambda k: (k, 0))
    whole = pl.BlockSpec(s.shape, lambda k: (0, 0))
    return pl.pallas_call(
        gradient_kernel,
        grid=(GRADIENT_STEPS,),
        in_specs=[pl.BlockSpec(stats.shape, lambda k: (0, 0, 0)), whole, whole, head, head],
        out_specs=[
            pl.BlockSpec((rows, depth), lambda k: (0, k)),
            pl.BlockSpec((copies, 128), lambda k: (0, 0)),
        ],
        out_shape=[
            pltpu.HBM((rows, width), BF),
            jax.ShapeDtypeStruct((copies, 128), F32),
        ],
        scratch_shapes=[pltpu.VMEM(s.shape, BF)],
        compiler_params=pltpu.CompilerParams(vmem_limit_bytes=VMEM_LIMIT),
        cost_estimate=pl.CostEstimate(
            flops=4 * rows * width * block, bytes_accessed=7 * 2**20, transcendentals=2**17
        ),
        name="gradient",
    )(stats, s, d, *heads)


def body(student_hidden, teacher_hidden, packing, token_mask, student_head, teacher_head, loss_scale):
    tok, width = student_hidden.shape
    n_dp, n_y = lax.axis_size("dp"), lax.axis_size("y")
    cap = max(2, 2 * tok // n_dp)
    rows = n_y * tok
    swap = [(0, 1), (1, 0)]

    destination = packing // (n_y * CORES * tok)
    local = packing % tok
    index = jnp.arange(tok, dtype=jnp.int32)
    earlier = (destination[:, None] == destination[None, :]) & (index[None, :] < index[:, None])
    rank = jnp.sum(earlier.astype(jnp.int32), axis=1)
    position = destination * cap + rank
    payload = jnp.concatenate(
        [teacher_hidden, jnp.broadcast_to((local + 1).astype(BF)[:, None], (tok, 128))], axis=1
    )

    def teacher_turn(_, carry):
        position, out, *_ = carry
        spread = (jnp.arange(n_dp * cap, dtype=jnp.int32)[:, None] == position[None, :]).astype(BF)
        send = dot(spread, payload, 1, 0).astype(BF)
        got = exchange(send.reshape(n_dp, cap, width + 128), "dp").reshape(n_dp * cap, width + 128)
        slots = got[:, width].astype(jnp.int32) - 1
        place = (index[:, None] == slots[None, :]).astype(BF)
        placed = dot(place, got[:, :width], 1, 0).astype(BF)
        heads, placed = lax.optimization_barrier(((student_head, teacher_head), placed))
        other = [lax.ppermute(head, "core", swap) for head in heads]
        out, other = ring_gather(placed, out, "y", other)
        return slots[:tok], out, *other

    student_rows = lax.all_gather(student_hidden, "y", axis=0)
    once = lax.optimization_barrier(jnp.int32(1))
    empty = buffers((n_y, tok, width), student_head.shape, teacher_head.shape)
    _, teacher_rows, *other = lax.fori_loop(0, once, teacher_turn, (position, *empty))

    mine = jnp.arange(rows, dtype=jnp.int32) // tok == lax.axis_index("y")
    mask = jnp.where(mine, jnp.tile(token_mask.astype(F32), n_y), 0.0)[None]

    s, d, stats = logits(student_rows, teacher_rows, (student_head, other[0], teacher_head, other[1]), mask)
    stats = exchange(stats, "y")
    partial, parts = gradient(stats, s, d, (student_head, other[0]), n_dp * CORES)
    summed = lax.psum_scatter(partial, "y", scatter_dimension=0, tiled=True)

    totals = jnp.sum(exchange(parts[:, None], ("dp", "core")), axis=(0, 1))
    counted = totals[1]
    loss = totals[0] / counted
    factor = loss_scale * token_mask.astype(F32) / counted
    hidden_grad = (factor[:, None] * summed.astype(F32)).astype(BF)
    return hidden_grad, loss


def solution(mesh):
    dp, vocab = mesh.devices.shape
    grid = Mesh(mesh.devices.reshape(dp, vocab // CORES, CORES), ("dp", "y", "core"))
    every = ("dp", "y", "core")
    return jax.shard_map(
        body,
        mesh=grid,
        in_specs=(
            P(every, None),
            P(every, None),
            P(every),
            P(every),
            P(None, ("y", "core")),
            P(None, ("y", "core")),
            P(),
        ),
        out_specs=(P(every, None), P()),
        check_vma=False,
    )
```

```python
import jax
import jax.experimental.pallas as pl
import jax.experimental.pallas.tpu as pltpu
import jax.numpy as jnp
from jax import lax
from jax.sharding import Mesh, PartitionSpec as P

BF = jnp.bfloat16
F32 = jnp.float32
CORES = 2
STATS = 8
STEPS = 4
LOGITS_VMEM = 24 * 1024 * 1024
GRADIENT_STEPS = 2
VMEM_LIMIT = 16 * 1024 * 1024


def dot(a, b, ca, cb):
    return lax.dot_general(a, b, (((ca,), (cb,)), ((), ())), preferred_element_type=F32)


def exchange(x, axis):
    return lax.all_to_all(x, axis, split_axis=0, concat_axis=0, tiled=True)


def ring_gather(x, out, axis, beside):
    n = lax.axis_size(axis)
    me = lax.axis_index(axis)
    right = [(i, (i + 1) % n) for i in range(n)]
    left = [(i, (i - 1) % n) for i in range(n)]
    half = x.shape[0] // 2

    def put(out, block, owner, row=0):
        return lax.dynamic_update_slice(out, block[None], (lax.rem(owner, n), row, 0))

    out = put(out, x, me)
    r = l = x
    for k in range(1, n // 2):
        r = lax.ppermute(r, axis, right)
        l = lax.ppermute(l, axis, left)
        out = put(out, r, me + n - k)
        out = put(out, l, me + k)
        if k == 2:
            r, l, beside = lax.optimization_barrier((r, l, beside))
    r = lax.ppermute(r[:half], axis, right)
    l = lax.ppermute(l[half:], axis, left)
    out = put(out, r, me + n // 2)
    return put(out, l, me + n // 2, half), beside


def buffers(near, *far):
    return pl.pallas_call(
        lambda *refs: None,
        out_specs=[pl.BlockSpec(memory_space=pltpu.VMEM)] + [pl.BlockSpec(memory_space=pl.ANY)] * len(far),
        out_shape=[pltpu.VMEM(near, BF)] + [pltpu.HBM(shape, BF) for shape in far],
        compiler_params=pltpu.CompilerParams(vmem_limit_bytes=VMEM_LIMIT),
        name="buffers",
    )()


def logits_kernel(me_ref, xs, xt, ws0, ws1, wt0, wt1, mask_ref, s_ref, d_ref, stats_ref, *scratch):
    *held, sems = scratch
    n_y, tok, width = xs.shape
    rows, block = n_y * tok, ws0.shape[1]
    depth = width // STEPS

    def copies(side, k):
        part = pl.ds(k * depth, depth)
        for j, ref in enumerate(((xs, ws0, ws1), (xt, wt0, wt1))[side]):
            at = (slice(None), slice(None), part) if j == 0 else (part, slice(None))
            yield pltpu.make_async_copy(ref.at[at], held[3 * side + j].at[at], sems.at[3 * side + j, k])

    for side in range(2):
        for k in range(STEPS):
            for copy in copies(side, k):
                copy.start()

    def product(side, out_ref):
        x, w0, w1 = held[3 * side : 3 * side + 3]
        for k in range(STEPS):
            for copy in copies(side, k):
                copy.wait()
            part = pl.ds(k * depth, depth)
            rows_in = x[:, :, part].reshape(rows, depth)
            p0, p1 = dot(rows_in, w0[part, :], 1, 0), dot(rows_in, w1[part, :], 1, 0)
            if k == 0:
                out_ref[:, :block] = p0
                out_ref[:, block:] = p1
            else:
                out_ref[:, :block] += p0
                out_ref[:, block:] += p1

    product(0, s_ref)
    s = s_ref[...]
    s_top = jnp.max(s, axis=1, keepdims=True)
    s_sum = jnp.sum(jnp.exp(s - s_top), axis=1, keepdims=True)
    product(1, d_ref)
    s, t = s_ref[...], d_ref[...]
    d = s - t
    d_ref[...] = d
    t_top = jnp.max(t, axis=1, keepdims=True)
    t_sum = jnp.sum(jnp.exp(t - t_top), axis=1, keepdims=True)
    cross = jnp.sum(jnp.exp(s - s_top) * d, axis=1, keepdims=True)
    columns = (s_top, t_top, s_sum, t_sum, cross)
    lane = lax.broadcasted_iota(jnp.int32, (rows, 128), 1)
    table = jnp.zeros((rows, 128), F32)
    for j, column in enumerate(columns):
        table = jnp.where(lane == j, column, table)
    table = table.T[:STATS]
    line = lax.broadcasted_iota(jnp.int32, (STATS, rows), 0)
    mask = jnp.concatenate([mask_ref[...].astype(F32)] * n_y, axis=1)
    mine = lax.div(lax.broadcasted_iota(jnp.int32, (1, rows), 1), tok) == me_ref[0]
    table = jnp.where(line == len(columns), jnp.where(mine, mask, 0.0), table)
    stats_ref[...] = jnp.broadcast_to(table[None], stats_ref.shape)


def logits(me, student_rows, teacher_rows, heads, mask):
    n_y, tok, width = student_rows.shape
    rows, block = n_y * tok, heads[0].shape[1]
    far, near = pl.BlockSpec(memory_space=pltpu.HBM), pl.BlockSpec(memory_space=pltpu.VMEM)
    side = [pltpu.VMEM(student_rows.shape, BF), pltpu.VMEM((width, block), BF), pltpu.VMEM((width, block), BF)]
    return pl.pallas_call(
        logits_kernel,
        in_specs=[pl.BlockSpec(memory_space=pltpu.SMEM)] + [far] * 6 + [near],
        out_specs=[near] * 3,
        out_shape=[
            jax.ShapeDtypeStruct((rows, CORES * block), F32),
            jax.ShapeDtypeStruct((rows, CORES * block), F32),
            jax.ShapeDtypeStruct((n_y, STATS, rows), F32),
        ],
        scratch_shapes=side + side + [pltpu.SemaphoreType.DMA((6, STEPS))],
        compiler_params=pltpu.CompilerParams(vmem_limit_bytes=LOGITS_VMEM),
        cost_estimate=pl.CostEstimate(
            flops=8 * rows * width * block, bytes_accessed=12 * 2**20, transcendentals=2**18
        ),
        name="logits",
    )(me, pltpu.with_memory_space_constraint(student_rows, pltpu.HBM), teacher_rows, *(pltpu.with_memory_space_constraint(x, pltpu.HBM) for x in heads), mask)


def gradient_kernel(stats_ref, s_ref, d_ref, w0_ref, w1_ref, out_ref, parts_ref, grad_ref):
    rows, block = s_ref.shape[0], w0_ref.shape[1]

    @pl.when(pl.program_id(0) == 0)
    def _():
        stats = [stats_ref[:, j, :] for j in range(6)]
        s_top = jnp.max(stats[0], axis=0, keepdims=True)
        t_top = jnp.max(stats[1], axis=0, keepdims=True)
        scale = jnp.exp(stats[0] - s_top)
        s_sum = jnp.sum(stats[2] * scale, axis=0, keepdims=True)
        t_sum = jnp.sum(stats[3] * jnp.exp(stats[1] - t_top), axis=0, keepdims=True)
        mean = jnp.sum(stats[4] * scale, axis=0, keepdims=True) / s_sum
        weights = jnp.sum(stats[5], axis=0, keepdims=True)
        row_kl = mean - (s_top + jnp.log(s_sum)) + (t_top + jnp.log(t_sum))
        lane = lax.broadcasted_iota(jnp.int32, parts_ref.shape, 1)
        parts_ref[...] = jnp.where(
            lane == 0, jnp.sum(weights * row_kl), jnp.where(lane == 1, jnp.sum(weights), 0.0)
        )
        line = lax.broadcasted_iota(jnp.int32, (128, rows), 0)
        table = jnp.where(line == 0, s_top, jnp.where(line == 1, 1.0 / s_sum, mean)).T
        probs = jnp.exp(s_ref[...] - table[:, 0:1]) * table[:, 1:2]
        grad_ref[...] = (probs * (d_ref[...] - table[:, 2:3])).astype(BF)

    out_ref[...] = (
        dot(grad_ref[:, :block], w0_ref[...], 1, 1) + dot(grad_ref[:, block:], w1_ref[...], 1, 1)
    ).astype(BF)


def gradient(stats, s, d, heads, copies):
    rows, (width, block) = s.shape[0], heads[0].shape
    depth = width // GRADIENT_STEPS
    head = pl.BlockSpec((depth, block), lambda k: (k, 0))
    whole = pl.BlockSpec(s.shape, lambda k: (0, 0))
    return pl.pallas_call(
        gradient_kernel,
        grid=(GRADIENT_STEPS,),
        in_specs=[pl.BlockSpec(stats.shape, lambda k: (0, 0, 0)), whole, whole, head, head],
        out_specs=[
            pl.BlockSpec((rows, depth), lambda k: (0, k)),
            pl.BlockSpec((copies, 128), lambda k: (0, 0)),
        ],
        out_shape=[
            pltpu.HBM((rows, width), BF),
            jax.ShapeDtypeStruct((copies, 128), F32),
        ],
        scratch_shapes=[pltpu.VMEM(s.shape, BF)],
        compiler_params=pltpu.CompilerParams(vmem_limit_bytes=VMEM_LIMIT),
        cost_estimate=pl.CostEstimate(
            flops=4 * rows * width * block, bytes_accessed=7 * 2**20, transcendentals=2**17
        ),
        name="gradient",
    )(stats, s, d, *heads)


def body(student_hidden, teacher_hidden, packing, token_mask, student_head, teacher_head, loss_scale):
    tok, width = student_hidden.shape
    n_dp, n_y = lax.axis_size("dp"), lax.axis_size("y")
    cap = max(2, 2 * tok // n_dp)
    rows = n_y * tok
    swap = [(0, 1), (1, 0)]

    destination = packing // (n_y * CORES * tok)
    local = packing % tok
    index = jnp.arange(tok, dtype=jnp.int32)
    earlier = (destination[:, None] == destination[None, :]) & (index[None, :] < index[:, None])
    rank = jnp.sum(earlier.astype(jnp.int32), axis=1)
    position = destination * cap + rank
    payload = jnp.concatenate(
        [teacher_hidden, jnp.broadcast_to((local + 1).astype(BF)[:, None], (tok, 128))], axis=1
    )

    def teacher_turn(_, carry):
        position, out, *_ = carry
        spread = (jnp.arange(n_dp * cap, dtype=jnp.int32)[:, None] == position[None, :]).astype(BF)
        send = dot(spread, payload, 1, 0).astype(BF)
        got = exchange(send.reshape(n_dp, cap, width + 128), "dp").reshape(n_dp * cap, width + 128)
        slots = got[:, width].astype(jnp.int32) - 1
        place = (index[:, None] == slots[None, :]).astype(BF)
        placed = dot(place, got[:, :width], 1, 0).astype(BF)
        heads, placed = lax.optimization_barrier(((student_head, teacher_head), placed))
        other = [lax.ppermute(head, "core", swap) for head in heads]
        out, other = ring_gather(placed, out, "y", other)
        return slots[:tok], out, *other

    student_rows = lax.all_gather(student_hidden, "y", axis=0)
    once = lax.optimization_barrier(jnp.int32(1))
    empty = buffers((n_y, tok, width), student_head.shape, teacher_head.shape)
    _, teacher_rows, *other = lax.fori_loop(0, once, teacher_turn, (position, *empty))

    me = lax.axis_index("y")[None]
    s, d, stats = logits(
        me, student_rows, teacher_rows, (student_head, other[0], teacher_head, other[1]), token_mask[None]
    )
    stats = exchange(stats, "y")
    partial, parts = gradient(stats, s, d, (student_head, other[0]), n_dp * CORES)
    summed = lax.psum_scatter(partial, "y", scatter_dimension=0, tiled=True)

    totals = jnp.sum(exchange(parts[:, None], ("dp", "core")), axis=(0, 1))
    counted = totals[1]
    loss = totals[0] / counted
    factor = loss_scale * token_mask.astype(F32) / counted
    hidden_grad = (factor[:, None] * summed.astype(F32)).astype(BF)
    return hidden_grad, loss


def solution(mesh):
    dp, vocab = mesh.devices.shape
    grid = Mesh(mesh.devices.reshape(dp, vocab // CORES, CORES), ("dp", "y", "core"))
    every = ("dp", "y", "core")
    return jax.shard_map(
        body,
        mesh=grid,
        in_specs=(
            P(every, None),
            P(every, None),
            P(every),
            P(every),
            P(None, ("y", "core")),
            P(None, ("y", "core")),
            P(),
        ),
        out_specs=(P(every, None), P()),
        check_vma=False,
    )
```

```python
import jax
import jax.experimental.pallas as pl
import jax.experimental.pallas.tpu as pltpu
import jax.numpy as jnp
from jax import lax
from jax.sharding import Mesh, PartitionSpec as P

BF = jnp.bfloat16
F32 = jnp.float32
CORES = 2
STATS = 8
STEPS = 4
LOGITS_VMEM = 24 * 1024 * 1024
GRADIENT_STEPS = 2
VMEM_LIMIT = 16 * 1024 * 1024


def dot(a, b, ca, cb):
    return lax.dot_general(a, b, (((ca,), (cb,)), ((), ())), preferred_element_type=F32)


def exchange(x, axis):
    return lax.all_to_all(x, axis, split_axis=0, concat_axis=0, tiled=True)


def ring_gather(x, out, axis, beside):
    n = lax.axis_size(axis)
    me = lax.axis_index(axis)
    right = [(i, (i + 1) % n) for i in range(n)]
    left = [(i, (i - 1) % n) for i in range(n)]
    share = x.shape[1] * 5 // 8 // 128 * 128

    def put(out, block, owner, column=0):
        return lax.dynamic_update_slice(out, block[None], (lax.rem(owner, n), 0, column))

    out = put(out, x, me)
    r = l = x
    for k in range(1, n // 2):
        r = lax.ppermute(r, axis, right)
        l = lax.ppermute(l, axis, left)
        out = put(out, r, me + n - k)
        out = put(out, l, me + k)
        if k == 2:
            r, l, beside = lax.optimization_barrier((r, l, beside))
    r = lax.ppermute(r[:, :share], axis, right)
    l = lax.ppermute(l[:, share:], axis, left)
    out = put(out, r, me + n // 2)
    return put(out, l, me + n // 2, share), beside


def buffers(near, *far):
    return pl.pallas_call(
        lambda *refs: None,
        out_specs=[pl.BlockSpec(memory_space=pltpu.VMEM)] + [pl.BlockSpec(memory_space=pl.ANY)] * len(far),
        out_shape=[pltpu.VMEM(near, BF)] + [pltpu.HBM(shape, BF) for shape in far],
        compiler_params=pltpu.CompilerParams(vmem_limit_bytes=VMEM_LIMIT),
        name="buffers",
    )()


def logits_kernel(me_ref, xs, xt, ws0, ws1, wt0, wt1, mask_ref, s_ref, d_ref, stats_ref, *scratch):
    *held, sems = scratch
    held.insert(3, xt)
    n_y, tok, width = xs.shape
    rows, block = n_y * tok, ws0.shape[1]
    depth = width // STEPS

    def copies(side, k):
        part = pl.ds(k * depth, depth)
        for j, ref in enumerate(((xs, ws0, ws1), (xt, wt0, wt1))[side]):
            if ref is xt:
                continue
            at = (slice(None), slice(None), part) if j == 0 else (part, slice(None))
            yield pltpu.make_async_copy(ref.at[at], held[3 * side + j].at[at], sems.at[3 * side + j, k])

    for side in range(2):
        for k in range(STEPS):
            for copy in copies(side, k):
                copy.start()

    def product(side, out_ref):
        x, w0, w1 = held[3 * side : 3 * side + 3]
        for k in range(STEPS):
            for copy in copies(side, k):
                copy.wait()
            part = pl.ds(k * depth, depth)
            rows_in = x[:, :, part].reshape(rows, depth)
            p0, p1 = dot(rows_in, w0[part, :], 1, 0), dot(rows_in, w1[part, :], 1, 0)
            if k == 0:
                out_ref[:, :block] = p0
                out_ref[:, block:] = p1
            else:
                out_ref[:, :block] += p0
                out_ref[:, block:] += p1

    product(0, s_ref)
    s = s_ref[...]
    s_top = jnp.max(s, axis=1, keepdims=True)
    s_sum = jnp.sum(jnp.exp(s - s_top), axis=1, keepdims=True)
    product(1, d_ref)
    s, t = s_ref[...], d_ref[...]
    d = s - t
    d_ref[...] = d
    t_top = jnp.max(t, axis=1, keepdims=True)
    t_sum = jnp.sum(jnp.exp(t - t_top), axis=1, keepdims=True)
    cross = jnp.sum(jnp.exp(s - s_top) * d, axis=1, keepdims=True)
    columns = (s_top, t_top, s_sum, t_sum, cross)
    lane = lax.broadcasted_iota(jnp.int32, (rows, 128), 1)
    table = jnp.zeros((rows, 128), F32)
    for j, column in enumerate(columns):
        table = jnp.where(lane == j, column, table)
    table = table.T[:STATS]
    line = lax.broadcasted_iota(jnp.int32, (STATS, rows), 0)
    mask = jnp.concatenate([mask_ref[...].astype(F32)] * n_y, axis=1)
    mine = lax.div(lax.broadcasted_iota(jnp.int32, (1, rows), 1), tok) == me_ref[0]
    table = jnp.where(line == len(columns), jnp.where(mine, mask, 0.0), table)
    stats_ref[...] = jnp.broadcast_to(table[None], stats_ref.shape)


def logits(me, student_rows, teacher_rows, heads, mask):
    n_y, tok, width = student_rows.shape
    rows, block = n_y * tok, heads[0].shape[1]
    far, near = pl.BlockSpec(memory_space=pltpu.HBM), pl.BlockSpec(memory_space=pltpu.VMEM)
    side = [pltpu.VMEM(student_rows.shape, BF), pltpu.VMEM((width, block), BF), pltpu.VMEM((width, block), BF)]
    return pl.pallas_call(
        logits_kernel,
        in_specs=[pl.BlockSpec(memory_space=pltpu.SMEM), far, near] + [far] * 4 + [near],
        out_specs=[near] * 3,
        out_shape=[
            jax.ShapeDtypeStruct((rows, CORES * block), F32),
            jax.ShapeDtypeStruct((rows, CORES * block), F32),
            jax.ShapeDtypeStruct((n_y, STATS, rows), F32),
        ],
        scratch_shapes=side + side[1:] + [pltpu.SemaphoreType.DMA((6, STEPS))],
        compiler_params=pltpu.CompilerParams(vmem_limit_bytes=LOGITS_VMEM),
        cost_estimate=pl.CostEstimate(
            flops=8 * rows * width * block, bytes_accessed=12 * 2**20, transcendentals=2**18
        ),
        name="logits",
    )(me, pltpu.with_memory_space_constraint(student_rows, pltpu.HBM), teacher_rows, *(pltpu.with_memory_space_constraint(x, pltpu.HBM) for x in heads), mask)


def gradient_kernel(stats_ref, s_ref, d_ref, w0_ref, w1_ref, out_ref, parts_ref, grad_ref):
    rows, block = s_ref.shape[0], w0_ref.shape[1]

    @pl.when(pl.program_id(0) == 0)
    def _():
        stats = [stats_ref[:, j, :] for j in range(6)]
        s_top = jnp.max(stats[0], axis=0, keepdims=True)
        t_top = jnp.max(stats[1], axis=0, keepdims=True)
        scale = jnp.exp(stats[0] - s_top)
        s_sum = jnp.sum(stats[2] * scale, axis=0, keepdims=True)
        t_sum = jnp.sum(stats[3] * jnp.exp(stats[1] - t_top), axis=0, keepdims=True)
        mean = jnp.sum(stats[4] * scale, axis=0, keepdims=True) / s_sum
        weights = jnp.sum(stats[5], axis=0, keepdims=True)
        row_kl = mean - (s_top + jnp.log(s_sum)) + (t_top + jnp.log(t_sum))
        lane = lax.broadcasted_iota(jnp.int32, parts_ref.shape, 1)
        parts_ref[...] = jnp.where(
            lane == 0, jnp.sum(weights * row_kl), jnp.where(lane == 1, jnp.sum(weights), 0.0)
        )
        line = lax.broadcasted_iota(jnp.int32, (128, rows), 0)
        table = jnp.where(line == 0, s_top, jnp.where(line == 1, 1.0 / s_sum, mean)).T
        probs = jnp.exp(s_ref[...] - table[:, 0:1]) * table[:, 1:2]
        grad_ref[...] = (probs * (d_ref[...] - table[:, 2:3])).astype(BF)

    out_ref[...] = (
        dot(grad_ref[:, :block], w0_ref[...], 1, 1) + dot(grad_ref[:, block:], w1_ref[...], 1, 1)
    ).astype(BF)


def gradient(stats, s, d, heads, copies):
    rows, (width, block) = s.shape[0], heads[0].shape
    depth = width // GRADIENT_STEPS
    head = pl.BlockSpec((depth, block), lambda k: (k, 0))
    whole = pl.BlockSpec(s.shape, lambda k: (0, 0))
    return pl.pallas_call(
        gradient_kernel,
        grid=(GRADIENT_STEPS,),
        in_specs=[pl.BlockSpec(stats.shape, lambda k: (0, 0, 0)), whole, whole, head, head],
        out_specs=[
            pl.BlockSpec((rows, depth), lambda k: (0, k)),
            pl.BlockSpec((copies, 128), lambda k: (0, 0)),
        ],
        out_shape=[
            pltpu.HBM((rows, width), BF),
            jax.ShapeDtypeStruct((copies, 128), F32),
        ],
        scratch_shapes=[pltpu.VMEM(s.shape, BF)],
        compiler_params=pltpu.CompilerParams(vmem_limit_bytes=VMEM_LIMIT),
        cost_estimate=pl.CostEstimate(
            flops=4 * rows * width * block, bytes_accessed=7 * 2**20, transcendentals=2**17
        ),
        name="gradient",
    )(stats, s, d, *heads)


def body(student_hidden, teacher_hidden, packing, token_mask, student_head, teacher_head, loss_scale):
    tok, width = student_hidden.shape
    n_dp, n_y = lax.axis_size("dp"), lax.axis_size("y")
    cap = max(2, 2 * tok // n_dp)
    rows = n_y * tok
    swap = [(0, 1), (1, 0)]

    destination = packing // (n_y * CORES * tok)
    local = packing % tok
    index = jnp.arange(tok, dtype=jnp.int32)
    earlier = (destination[:, None] == destination[None, :]) & (index[None, :] < index[:, None])
    rank = jnp.sum(earlier.astype(jnp.int32), axis=1)
    position = destination * cap + rank
    payload = jnp.concatenate(
        [teacher_hidden, jnp.broadcast_to((local + 1).astype(BF)[:, None], (tok, 128))], axis=1
    )

    def teacher_turn(_, carry):
        position, out, *_ = carry
        spread = (jnp.arange(n_dp * cap, dtype=jnp.int32)[:, None] == position[None, :]).astype(BF)
        send = dot(spread, payload, 1, 0).astype(BF)
        got = exchange(send.reshape(n_dp, cap, width + 128), "dp").reshape(n_dp * cap, width + 128)
        slots = got[:, width].astype(jnp.int32) - 1
        place = (index[:, None] == slots[None, :]).astype(BF)
        placed = dot(place, got[:, :width], 1, 0).astype(BF)
        heads, placed = lax.optimization_barrier(((student_head, teacher_head), placed))
        other = [lax.ppermute(head, "core", swap) for head in heads]
        out, other = ring_gather(placed, out, "y", other)
        return slots[:tok], out, *other

    student_rows = lax.all_gather(student_hidden, "y", axis=0)
    once = lax.optimization_barrier(jnp.int32(1))
    empty = buffers((n_y, tok, width), student_head.shape, teacher_head.shape)
    _, teacher_rows, *other = lax.fori_loop(0, once, teacher_turn, (position, *empty))

    me = lax.axis_index("y")[None]
    s, d, stats = logits(
        me, student_rows, teacher_rows, (student_head, other[0], teacher_head, other[1]), token_mask[None]
    )
    stats = exchange(stats, "y")
    partial, parts = gradient(stats, s, d, (student_head, other[0]), n_dp * CORES)
    summed = lax.psum_scatter(partial, "y", scatter_dimension=0, tiled=True)

    totals = jnp.sum(exchange(parts[:, None], ("dp", "core")), axis=(0, 1))
    counted = totals[1]
    loss = totals[0] / counted
    factor = loss_scale * token_mask.astype(F32) / counted
    hidden_grad = (factor[:, None] * summed.astype(F32)).astype(BF)
    return hidden_grad, loss


def solution(mesh):
    dp, vocab = mesh.devices.shape
    grid = Mesh(mesh.devices.reshape(dp, vocab // CORES, CORES), ("dp", "y", "core"))
    every = ("dp", "y", "core")
    return jax.shard_map(
        body,
        mesh=grid,
        in_specs=(
            P(every, None),
            P(every, None),
            P(every),
            P(every),
            P(None, ("y", "core")),
            P(None, ("y", "core")),
            P(),
        ),
        out_specs=(P(every, None), P()),
        check_vma=False,
    )
```

```python
import jax
import jax.experimental.pallas as pl
import jax.experimental.pallas.tpu as pltpu
import jax.numpy as jnp
from jax import lax
from jax.sharding import Mesh, PartitionSpec as P

BF = jnp.bfloat16
F32 = jnp.float32
CORES = 2
STATS = 8
STEPS = 4
LOGITS_VMEM = 24 * 1024 * 1024
GRADIENT_STEPS = 2
VMEM_LIMIT = 16 * 1024 * 1024


def dot(a, b, ca, cb):
    return lax.dot_general(a, b, (((ca,), (cb,)), ((), ())), preferred_element_type=F32)


def exchange(x, axis):
    return lax.all_to_all(x, axis, split_axis=0, concat_axis=0, tiled=True)


def ring_gather(x, out, axis, beside):
    n = lax.axis_size(axis)
    me = lax.axis_index(axis)
    right = [(i, (i + 1) % n) for i in range(n)]
    left = [(i, (i - 1) % n) for i in range(n)]
    share = x.shape[1] * 5 // 8 // 128 * 128

    def put(out, block, owner, column=0):
        return lax.dynamic_update_slice(out, block[None], (lax.rem(owner, n), 0, column))

    out = put(out, x, me)
    r = l = x
    for k in range(1, n // 2):
        r = lax.ppermute(r, axis, right)
        l = lax.ppermute(l, axis, left)
        out = put(out, r, me + n - k)
        out = put(out, l, me + k)
        if k == 1:
            r, l, beside = lax.optimization_barrier((r, l, beside))
    r = lax.ppermute(r[:, :share], axis, right)
    l = lax.ppermute(l[:, share:], axis, left)
    out = put(out, r, me + n // 2)
    return put(out, l, me + n // 2, share), beside


def buffers(near, *far):
    return pl.pallas_call(
        lambda *refs: None,
        out_specs=[pl.BlockSpec(memory_space=pltpu.VMEM)] + [pl.BlockSpec(memory_space=pl.ANY)] * len(far),
        out_shape=[pltpu.VMEM(near, BF)] + [pltpu.HBM(shape, BF) for shape in far],
        compiler_params=pltpu.CompilerParams(vmem_limit_bytes=VMEM_LIMIT),
        name="buffers",
    )()


def logits_kernel(me_ref, xs, xt, ws0, ws1, wt0, wt1, mask_ref, s_ref, d_ref, stats_ref, ws0_out, ws1_out, *scratch):
    xs_in, wt0_in, wt1_in, sems = scratch
    held = [xs_in, ws0_out, ws1_out, xt, wt0_in, wt1_in]
    n_y, tok, width = xs.shape
    rows, block = n_y * tok, ws0.shape[1]
    depth = width // STEPS

    def copies(side, k):
        part = pl.ds(k * depth, depth)
        for j, ref in enumerate(((xs, ws0, ws1), (xt, wt0, wt1))[side]):
            if ref is xt:
                continue
            at = (slice(None), slice(None), part) if j == 0 else (part, slice(None))
            yield pltpu.make_async_copy(ref.at[at], held[3 * side + j].at[at], sems.at[3 * side + j, k])

    for side in range(2):
        for k in range(STEPS):
            for copy in copies(side, k):
                copy.start()

    def product(side, out_ref):
        x, w0, w1 = held[3 * side : 3 * side + 3]
        for k in range(STEPS):
            for copy in copies(side, k):
                copy.wait()
            part = pl.ds(k * depth, depth)
            rows_in = x[:, :, part].reshape(rows, depth)
            p0, p1 = dot(rows_in, w0[part, :], 1, 0), dot(rows_in, w1[part, :], 1, 0)
            if k == 0:
                out_ref[:, :block] = p0
                out_ref[:, block:] = p1
            else:
                out_ref[:, :block] += p0
                out_ref[:, block:] += p1

    product(0, s_ref)
    s = s_ref[...]
    s_top = jnp.max(s, axis=1, keepdims=True)
    s_sum = jnp.sum(jnp.exp(s - s_top), axis=1, keepdims=True)
    product(1, d_ref)
    s, t = s_ref[...], d_ref[...]
    d = s - t
    d_ref[...] = d
    t_top = jnp.max(t, axis=1, keepdims=True)
    t_sum = jnp.sum(jnp.exp(t - t_top), axis=1, keepdims=True)
    cross = jnp.sum(jnp.exp(s - s_top) * d, axis=1, keepdims=True)
    columns = (s_top, t_top, s_sum, t_sum, cross)
    lane = lax.broadcasted_iota(jnp.int32, (rows, 128), 1)
    table = jnp.zeros((rows, 128), F32)
    for j, column in enumerate(columns):
        table = jnp.where(lane == j, column, table)
    table = table.T[:STATS]
    line = lax.broadcasted_iota(jnp.int32, (STATS, rows), 0)
    mask = jnp.concatenate([mask_ref[...].astype(F32)] * n_y, axis=1)
    mine = lax.div(lax.broadcasted_iota(jnp.int32, (1, rows), 1), tok) == me_ref[0]
    table = jnp.where(line == len(columns), jnp.where(mine, mask, 0.0), table)
    stats_ref[...] = jnp.broadcast_to(table[None], stats_ref.shape)


def logits(me, student_rows, teacher_rows, heads, mask):
    n_y, tok, width = student_rows.shape
    rows, block = n_y * tok, heads[0].shape[1]
    far, near = pl.BlockSpec(memory_space=pltpu.HBM), pl.BlockSpec(memory_space=pltpu.VMEM)
    side = [pltpu.VMEM(student_rows.shape, BF), pltpu.VMEM((width, block), BF), pltpu.VMEM((width, block), BF)]
    return pl.pallas_call(
        logits_kernel,
        in_specs=[pl.BlockSpec(memory_space=pltpu.SMEM), far, near] + [far] * 4 + [near],
        out_specs=[near] * 5,
        out_shape=[
            jax.ShapeDtypeStruct((rows, CORES * block), F32),
            jax.ShapeDtypeStruct((rows, CORES * block), F32),
            jax.ShapeDtypeStruct((n_y, STATS, rows), F32),
            pltpu.VMEM((width, block), BF),
            pltpu.VMEM((width, block), BF),
        ],
        scratch_shapes=side + [pltpu.SemaphoreType.DMA((6, STEPS))],
        compiler_params=pltpu.CompilerParams(vmem_limit_bytes=LOGITS_VMEM),
        cost_estimate=pl.CostEstimate(
            flops=8 * rows * width * block, bytes_accessed=12 * 2**20, transcendentals=2**18
        ),
        name="logits",
    )(me, pltpu.with_memory_space_constraint(student_rows, pltpu.HBM), teacher_rows, *(pltpu.with_memory_space_constraint(x, pltpu.HBM) for x in heads), mask)


def gradient_kernel(stats_ref, s_ref, d_ref, w0_ref, w1_ref, out_ref, parts_ref, grad_ref):
    rows, block = s_ref.shape[0], w0_ref.shape[1]

    @pl.when(pl.program_id(0) == 0)
    def _():
        stats = [stats_ref[:, j, :] for j in range(6)]
        s_top = jnp.max(stats[0], axis=0, keepdims=True)
        t_top = jnp.max(stats[1], axis=0, keepdims=True)
        scale = jnp.exp(stats[0] - s_top)
        s_sum = jnp.sum(stats[2] * scale, axis=0, keepdims=True)
        t_sum = jnp.sum(stats[3] * jnp.exp(stats[1] - t_top), axis=0, keepdims=True)
        mean = jnp.sum(stats[4] * scale, axis=0, keepdims=True) / s_sum
        weights = jnp.sum(stats[5], axis=0, keepdims=True)
        row_kl = mean - (s_top + jnp.log(s_sum)) + (t_top + jnp.log(t_sum))
        lane = lax.broadcasted_iota(jnp.int32, parts_ref.shape, 1)
        parts_ref[...] = jnp.where(
            lane == 0, jnp.sum(weights * row_kl), jnp.where(lane == 1, jnp.sum(weights), 0.0)
        )
        line = lax.broadcasted_iota(jnp.int32, (128, rows), 0)
        table = jnp.where(line == 0, s_top, jnp.where(line == 1, 1.0 / s_sum, mean)).T
        probs = jnp.exp(s_ref[...] - table[:, 0:1]) * table[:, 1:2]
        grad_ref[...] = (probs * (d_ref[...] - table[:, 2:3])).astype(BF)

    out_ref[...] = (
        dot(grad_ref[:, :block], w0_ref[...], 1, 1) + dot(grad_ref[:, block:], w1_ref[...], 1, 1)
    ).astype(BF)


def gradient(stats, s, d, heads, copies):
    rows, (width, block) = s.shape[0], heads[0].shape
    depth = width // GRADIENT_STEPS
    head = pl.BlockSpec((depth, block), lambda k: (k, 0))
    whole = pl.BlockSpec(s.shape, lambda k: (0, 0))
    return pl.pallas_call(
        gradient_kernel,
        grid=(GRADIENT_STEPS,),
        in_specs=[pl.BlockSpec(stats.shape, lambda k: (0, 0, 0)), whole, whole, head, head],
        out_specs=[
            pl.BlockSpec((rows, depth), lambda k: (0, k)),
            pl.BlockSpec((copies, 128), lambda k: (0, 0)),
        ],
        out_shape=[
            pltpu.HBM((rows, width), BF),
            jax.ShapeDtypeStruct((copies, 128), F32),
        ],
        scratch_shapes=[pltpu.VMEM(s.shape, BF)],
        compiler_params=pltpu.CompilerParams(vmem_limit_bytes=VMEM_LIMIT),
        cost_estimate=pl.CostEstimate(
            flops=4 * rows * width * block, bytes_accessed=7 * 2**20, transcendentals=2**17
        ),
        name="gradient",
    )(stats, s, d, *heads)


def body(student_hidden, teacher_hidden, packing, token_mask, student_head, teacher_head, loss_scale):
    tok, width = student_hidden.shape
    n_dp, n_y = lax.axis_size("dp"), lax.axis_size("y")
    cap = max(2, 2 * tok // n_dp)
    rows = n_y * tok
    swap = [(0, 1), (1, 0)]

    destination = packing // (n_y * CORES * tok)
    local = packing % tok
    index = jnp.arange(tok, dtype=jnp.int32)
    earlier = (destination[:, None] == destination[None, :]) & (index[None, :] < index[:, None])
    rank = jnp.sum(earlier.astype(jnp.int32), axis=1)
    position = destination * cap + rank
    payload = jnp.concatenate(
        [teacher_hidden, jnp.broadcast_to((local + 1).astype(BF)[:, None], (tok, 128))], axis=1
    )

    def teacher_turn(_, carry):
        position, out, *_ = carry
        spread = (jnp.arange(n_dp * cap, dtype=jnp.int32)[:, None] == position[None, :]).astype(BF)
        send = dot(spread, payload, 1, 0).astype(BF)
        heads, send = lax.optimization_barrier(((student_head, teacher_head), send))
        other = [lax.ppermute(head, "core", swap) for head in heads]
        got = exchange(send.reshape(n_dp, cap, width + 128), "dp").reshape(n_dp * cap, width + 128)
        slots = got[:, width].astype(jnp.int32) - 1
        place = (index[:, None] == slots[None, :]).astype(BF)
        placed = dot(place, got[:, :width], 1, 0).astype(BF)
        out, other = ring_gather(placed, out, "y", other)
        return slots[:tok], out, *other

    student_rows = lax.all_gather(student_hidden, "y", axis=0)
    once = lax.optimization_barrier(jnp.int32(1))
    empty = buffers((n_y, tok, width), student_head.shape, teacher_head.shape)
    _, teacher_rows, *other = lax.fori_loop(0, once, teacher_turn, (position, *empty))

    me = lax.axis_index("y")[None]
    s, d, stats, *near_heads = logits(
        me, student_rows, teacher_rows, (student_head, other[0], teacher_head, other[1]), token_mask[None]
    )
    stats = exchange(stats, "y")
    partial, parts = gradient(stats, s, d, near_heads, n_dp * CORES)
    summed = lax.psum_scatter(partial, "y", scatter_dimension=0, tiled=True)

    totals = jnp.sum(exchange(parts[:, None], ("dp", "core")), axis=(0, 1))
    counted = totals[1]
    loss = totals[0] / counted
    factor = loss_scale * token_mask.astype(F32) / counted
    hidden_grad = (factor[:, None] * summed.astype(F32)).astype(BF)
    return hidden_grad, loss


def solution(mesh):
    dp, vocab = mesh.devices.shape
    grid = Mesh(mesh.devices.reshape(dp, vocab // CORES, CORES), ("dp", "y", "core"))
    every = ("dp", "y", "core")
    return jax.shard_map(
        body,
        mesh=grid,
        in_specs=(
            P(every, None),
            P(every, None),
            P(every),
            P(every),
            P(None, ("y", "core")),
            P(None, ("y", "core")),
            P(),
        ),
        out_specs=(P(every, None), P()),
        check_vma=False,
    )
```

```python
import jax
import jax.experimental.pallas as pl
import jax.experimental.pallas.tpu as pltpu
import jax.numpy as jnp
from jax import lax
from jax.sharding import Mesh, PartitionSpec as P

BF = jnp.bfloat16
F32 = jnp.float32
CORES = 2
STATS = 8
STEPS = 4
LOGITS_VMEM = 24 * 1024 * 1024
GRADIENT_STEPS = 2
VMEM_LIMIT = 16 * 1024 * 1024


def dot(a, b, ca, cb):
    return lax.dot_general(a, b, (((ca,), (cb,)), ((), ())), preferred_element_type=F32)


def exchange(x, axis):
    return lax.all_to_all(x, axis, split_axis=0, concat_axis=0, tiled=True)


def ring_gather(x, out, axis, beside):
    n = lax.axis_size(axis)
    me = lax.axis_index(axis)
    right = [(i, (i + 1) % n) for i in range(n)]
    left = [(i, (i - 1) % n) for i in range(n)]
    share = x.shape[1] * 3 // 4 // 128 * 128

    def put(out, block, owner, column=0):
        return lax.dynamic_update_slice(out, block[None], (lax.rem(owner, n), 0, column))

    out = put(out, x, me)
    r = l = x
    for k in range(1, n // 2):
        r = lax.ppermute(r, axis, right)
        l = lax.ppermute(l, axis, left)
        out = put(out, r, me + n - k)
        out = put(out, l, me + k)
        if k == 1:
            r, l, beside = lax.optimization_barrier((r, l, beside))
    r = lax.ppermute(r[:, :share], axis, right)
    l = lax.ppermute(l[:, share:], axis, left)
    out = put(out, r, me + n // 2)
    return put(out, l, me + n // 2, share), beside


def buffers(near, *far):
    return pl.pallas_call(
        lambda *refs: None,
        out_specs=[pl.BlockSpec(memory_space=pltpu.VMEM)] + [pl.BlockSpec(memory_space=pl.ANY)] * len(far),
        out_shape=[pltpu.VMEM(near, BF)] + [pltpu.HBM(shape, BF) for shape in far],
        compiler_params=pltpu.CompilerParams(vmem_limit_bytes=VMEM_LIMIT),
        name="buffers",
    )()


def logits_kernel(me_ref, xs, xt, ws0, ws1, wt0, wt1, mask_ref, s_ref, d_ref, stats_ref, ws0_out, ws1_out, *scratch):
    xs_in, wt0_in, wt1_in, sems = scratch
    held = [xs_in, ws0_out, ws1_out, xt, wt0_in, wt1_in]
    n_y, tok, width = xs.shape
    rows, block = n_y * tok, ws0.shape[1]
    depth = width // STEPS

    def copies(side, k):
        part = pl.ds(k * depth, depth)
        for j, ref in enumerate(((xs, ws0, ws1), (xt, wt0, wt1))[side]):
            if ref is xt:
                continue
            at = (slice(None), slice(None), part) if j == 0 else (part, slice(None))
            yield pltpu.make_async_copy(ref.at[at], held[3 * side + j].at[at], sems.at[3 * side + j, k])

    for side in range(2):
        for k in range(STEPS):
            for copy in copies(side, k):
                copy.start()

    def product(side, out_ref):
        x, w0, w1 = held[3 * side : 3 * side + 3]
        for k in range(STEPS):
            for copy in copies(side, k):
                copy.wait()
            part = pl.ds(k * depth, depth)
            rows_in = x[:, :, part].reshape(rows, depth)
            p0, p1 = dot(rows_in, w0[part, :], 1, 0), dot(rows_in, w1[part, :], 1, 0)
            if k == 0:
                out_ref[:, :block] = p0
                out_ref[:, block:] = p1
            else:
                out_ref[:, :block] += p0
                out_ref[:, block:] += p1

    product(0, s_ref)
    s = s_ref[...]
    s_top = jnp.max(s, axis=1, keepdims=True)
    s_sum = jnp.sum(jnp.exp(s - s_top), axis=1, keepdims=True)
    product(1, d_ref)
    s, t = s_ref[...], d_ref[...]
    d = s - t
    d_ref[...] = d
    t_top = jnp.max(t, axis=1, keepdims=True)
    t_sum = jnp.sum(jnp.exp(t - t_top), axis=1, keepdims=True)
    cross = jnp.sum(jnp.exp(s - s_top) * d, axis=1, keepdims=True)
    columns = (s_top, t_top, s_sum, t_sum, cross)
    lane = lax.broadcasted_iota(jnp.int32, (rows, 128), 1)
    table = jnp.zeros((rows, 128), F32)
    for j, column in enumerate(columns):
        table = jnp.where(lane == j, column, table)
    table = table.T[:STATS]
    line = lax.broadcasted_iota(jnp.int32, (STATS, rows), 0)
    mask = jnp.concatenate([mask_ref[...].astype(F32)] * n_y, axis=1)
    mine = lax.div(lax.broadcasted_iota(jnp.int32, (1, rows), 1), tok) == me_ref[0]
    table = jnp.where(line == len(columns), jnp.where(mine, mask, 0.0), table)
    stats_ref[...] = jnp.broadcast_to(table[None], stats_ref.shape)


def logits(me, student_rows, teacher_rows, heads, mask):
    n_y, tok, width = student_rows.shape
    rows, block = n_y * tok, heads[0].shape[1]
    far, near = pl.BlockSpec(memory_space=pltpu.HBM), pl.BlockSpec(memory_space=pltpu.VMEM)
    side = [pltpu.VMEM(student_rows.shape, BF), pltpu.VMEM((width, block), BF), pltpu.VMEM((width, block), BF)]
    return pl.pallas_call(
        logits_kernel,
        in_specs=[pl.BlockSpec(memory_space=pltpu.SMEM), far, near] + [far] * 4 + [near],
        out_specs=[near] * 5,
        out_shape=[
            jax.ShapeDtypeStruct((rows, CORES * block), F32),
            jax.ShapeDtypeStruct((rows, CORES * block), F32),
            jax.ShapeDtypeStruct((n_y, STATS, rows), F32),
            pltpu.VMEM((width, block), BF),
            pltpu.VMEM((width, block), BF),
        ],
        scratch_shapes=side + [pltpu.SemaphoreType.DMA((6, STEPS))],
        compiler_params=pltpu.CompilerParams(vmem_limit_bytes=LOGITS_VMEM),
        cost_estimate=pl.CostEstimate(
            flops=8 * rows * width * block, bytes_accessed=12 * 2**20, transcendentals=2**18
        ),
        name="logits",
    )(me, pltpu.with_memory_space_constraint(student_rows, pltpu.HBM), teacher_rows, *(pltpu.with_memory_space_constraint(x, pltpu.HBM) for x in heads), mask)


def gradient_kernel(stats_ref, s_ref, d_ref, w0_ref, w1_ref, out_ref, parts_ref, grad_ref):
    rows, block = s_ref.shape[0], w0_ref.shape[1]

    @pl.when(pl.program_id(0) == 0)
    def _():
        stats = [stats_ref[:, j, :] for j in range(6)]
        s_top = jnp.max(stats[0], axis=0, keepdims=True)
        t_top = jnp.max(stats[1], axis=0, keepdims=True)
        scale = jnp.exp(stats[0] - s_top)
        s_sum = jnp.sum(stats[2] * scale, axis=0, keepdims=True)
        t_sum = jnp.sum(stats[3] * jnp.exp(stats[1] - t_top), axis=0, keepdims=True)
        mean = jnp.sum(stats[4] * scale, axis=0, keepdims=True) / s_sum
        weights = jnp.sum(stats[5], axis=0, keepdims=True)
        row_kl = mean - (s_top + jnp.log(s_sum)) + (t_top + jnp.log(t_sum))
        lane = lax.broadcasted_iota(jnp.int32, parts_ref.shape, 1)
        parts_ref[...] = jnp.where(
            lane == 0, jnp.sum(weights * row_kl), jnp.where(lane == 1, jnp.sum(weights), 0.0)
        )
        line = lax.broadcasted_iota(jnp.int32, (128, rows), 0)
        table = jnp.where(line == 0, s_top, jnp.where(line == 1, 1.0 / s_sum, mean)).T
        probs = jnp.exp(s_ref[...] - table[:, 0:1]) * table[:, 1:2]
        grad_ref[...] = (probs * (d_ref[...] - table[:, 2:3])).astype(BF)

    out_ref[...] = (
        dot(grad_ref[:, :block], w0_ref[...], 1, 1) + dot(grad_ref[:, block:], w1_ref[...], 1, 1)
    ).astype(BF)


def gradient(stats, s, d, heads, copies):
    rows, (width, block) = s.shape[0], heads[0].shape
    depth = width // GRADIENT_STEPS
    head = pl.BlockSpec((depth, block), lambda k: (k, 0))
    whole = pl.BlockSpec(s.shape, lambda k: (0, 0))
    return pl.pallas_call(
        gradient_kernel,
        grid=(GRADIENT_STEPS,),
        in_specs=[pl.BlockSpec(stats.shape, lambda k: (0, 0, 0)), whole, whole, head, head],
        out_specs=[
            pl.BlockSpec((rows, depth), lambda k: (0, k)),
            pl.BlockSpec((copies, 128), lambda k: (0, 0)),
        ],
        out_shape=[
            pltpu.HBM((rows, width), BF),
            jax.ShapeDtypeStruct((copies, 128), F32),
        ],
        scratch_shapes=[pltpu.VMEM(s.shape, BF)],
        compiler_params=pltpu.CompilerParams(vmem_limit_bytes=VMEM_LIMIT),
        cost_estimate=pl.CostEstimate(
            flops=4 * rows * width * block, bytes_accessed=7 * 2**20, transcendentals=2**17
        ),
        name="gradient",
    )(stats, s, d, *heads)


def body(student_hidden, teacher_hidden, packing, token_mask, student_head, teacher_head, loss_scale):
    tok, width = student_hidden.shape
    n_dp, n_y = lax.axis_size("dp"), lax.axis_size("y")
    cap = max(2, 2 * tok // n_dp)
    rows = n_y * tok
    swap = [(0, 1), (1, 0)]

    destination = packing // (n_y * CORES * tok)
    local = packing % tok
    index = jnp.arange(tok, dtype=jnp.int32)
    earlier = (destination[:, None] == destination[None, :]) & (index[None, :] < index[:, None])
    rank = jnp.sum(earlier.astype(jnp.int32), axis=1)
    position = destination * cap + rank
    payload = jnp.concatenate(
        [teacher_hidden, jnp.broadcast_to((local + 1).astype(BF)[:, None], (tok, 128))], axis=1
    )

    def teacher_turn(_, carry):
        position, out, *_ = carry
        spread = (jnp.arange(n_dp * cap, dtype=jnp.int32)[:, None] == position[None, :]).astype(BF)
        send = dot(spread, payload, 1, 0).astype(BF)
        heads, send = lax.optimization_barrier(((student_head, teacher_head), send))
        other = [lax.ppermute(head, "core", swap) for head in heads]
        got = exchange(send.reshape(n_dp, cap, width + 128), "dp").reshape(n_dp * cap, width + 128)
        slots = got[:, width].astype(jnp.int32) - 1
        place = (index[:, None] == slots[None, :]).astype(BF)
        placed = dot(place, got[:, :width], 1, 0).astype(BF)
        out, other = ring_gather(placed, out, "y", other)
        return slots[:tok], out, *other

    student_rows = lax.all_gather(student_hidden, "y", axis=0)
    once = lax.optimization_barrier(jnp.int32(1))
    empty = buffers((n_y, tok, width), student_head.shape, teacher_head.shape)
    _, teacher_rows, *other = lax.fori_loop(0, once, teacher_turn, (position, *empty))

    me = lax.axis_index("y")[None]
    s, d, stats, *near_heads = logits(
        me, student_rows, teacher_rows, (student_head, other[0], teacher_head, other[1]), token_mask[None]
    )
    stats = exchange(stats, "y")
    partial, parts = gradient(stats, s, d, near_heads, n_dp * CORES)
    summed = lax.psum_scatter(partial, "y", scatter_dimension=0, tiled=True)

    totals = jnp.sum(exchange(parts[:, None], ("dp", "core")), axis=(0, 1))
    counted = totals[1]
    loss = totals[0] / counted
    factor = loss_scale * token_mask.astype(F32) / counted
    hidden_grad = (factor[:, None] * summed.astype(F32)).astype(BF)
    return hidden_grad, loss


def solution(mesh):
    dp, vocab = mesh.devices.shape
    grid = Mesh(mesh.devices.reshape(dp, vocab // CORES, CORES), ("dp", "y", "core"))
    every = ("dp", "y", "core")
    return jax.shard_map(
        body,
        mesh=grid,
        in_specs=(
            P(every, None),
            P(every, None),
            P(every),
            P(every),
            P(None, ("y", "core")),
            P(None, ("y", "core")),
            P(),
        ),
        out_specs=(P(every, None), P()),
        check_vma=False,
    )
```
